32 devices in a mesh: dp: 4 (over z), comp: 8 (over y, x, core).
Axes of the slice: x: 2, y: 2, z: 4, core: 2. Of those that a mesh axis runs over, the one named last changes fastest.
Arguments:
- vectors: bfloat16 [512, 256], P('dp'), may hold values from -8 to 8
- centers: float32 [128, 256], P('comp'), may hold values from -1.5 to 1.5
- factors: bfloat16 [128, 256, 256], P('comp', 'dp'), may hold values from -1 to 9.065873, as said below
- mixing: float32 [128], P('comp'), may hold values from 0.00234375 to 0.0234375
Outputs:
- new_factors: float32 [128, 256, 256], P('comp', 'dp')
- new_means: float32 [128, 256], P('comp')
- new_weights: float32 [128], P('comp')
- evidence: float32 [512], P('dp')
The draws below stay inside these ranges and needn't reach their ends.
Inputs may be any that keep to these rules, and one draw needn't show every extreme that they name: `factors`: each component's 256 x 256 factor is lower triangular with a positive diagonal.
All inputs are finite; a program needn't handle non-finite values.
Results may differ from the reference program's by a relative error of at most 0.0003.
Values may be sent and summed in bfloat16 or wider, within the bound.
A program may use at most 64 MiB of HBM per device.

```python
import math
import jax
import jax.numpy as jnp
from jax import lax

D = 256
VECTORS = 512
COMPONENTS = 128


def sharp_plan(key):
    plan_key = jax.random.fold_in(key, 71)
    picked = jax.random.permutation(plan_key, COMPONENTS)[:8]
    chosen = jax.random.permutation(jax.random.fold_in(plan_key, 1), VECTORS)[:4]
    return (picked, chosen)


def base_centers(key):
    center_key = jax.random.fold_in(key, 37)
    values = jnp.clip(jax.random.normal(center_key, (COMPONENTS, D)) * 0.5, -1.5, 1.5)
    picked, chosen = sharp_plan(key)
    values = values.at[picked[1::2]].set(values[picked[0::2]])
    return values.astype(jnp.float32)


def draw_centers(key, part):
    return base_centers(key)


def draw_vectors(key, part):
    first_key = jax.random.fold_in(jax.random.fold_in(key, 11), 0)
    values = jnp.clip(jax.random.normal(first_key, (VECTORS, D)), -5.0, 5.0)
    picked, chosen = sharp_plan(key)
    values = values.at[chosen].set(base_centers(key)[picked[0::2]])
    return values.astype(jnp.float32).astype(jnp.bfloat16)


def draw_factors(key, part):
    first_key, second_key = jax.random.split(jax.random.fold_in(key, 23))
    diag_lo, diag_hi, spread = (0.6, 1.6, 0.25)
    diagonal = jnp.exp(jax.random.uniform(first_key, (COMPONENTS, D), minval=math.log(diag_lo), maxval=math.log(diag_hi)))
    picked, chosen = sharp_plan(key)
    strength = jnp.array([1.0, 1.0, 1.2, 1.2, 1.4, 1.4, 1.0, 1.0], jnp.float32)
    log_sharp = jnp.broadcast_to((1.0 + 220.0 / D * strength)[:, None], (8, D))
    log_sharp = log_sharp.at[1::2, 0].add(-2.0)
    diagonal = diagonal.at[picked].set(jnp.exp(log_sharp))
    below = jnp.clip(jax.random.normal(second_key, (COMPONENTS, D, D)), -6.0, 6.0) * (spread / math.sqrt(D))
    lower_mask = jnp.tril(jnp.ones((D, D), jnp.float32), -1)
    values = below * lower_mask[None] + diagonal[:, :, None] * jnp.eye(D, dtype=jnp.float32)[None]
    return values.astype(jnp.float32).astype(jnp.bfloat16)


def level_of(stream_key, shape, cuts, least, high):
    factor_of, own = 1.0, jax.random.fold_in(stream_key, 6)
    for position, blocks in cuts:
        draws = jnp.exp(jax.random.uniform(jax.random.fold_in(own, position), (blocks,), jnp.float32, least / len(cuts), high / len(cuts)))
        factor_of = factor_of * jnp.repeat(draws, shape[position] // blocks).reshape([-1 if axis == position else 1 for axis in range(len(shape))])
    return factor_of


def setup_inputs(seed: int = 0) -> dict:
    seeds = jax.random.split(jax.random.key(seed), 5)
    return {
        "vectors": draw_vectors(jax.random.fold_in(seeds[4], 71), 0),
        "centers": draw_centers(jax.random.fold_in(seeds[4], 71), 0),
        "factors": draw_factors(jax.random.fold_in(seeds[4], 71), 0),
        "mixing": jnp.clip(jnp.exp(math.log(0.0234375) - 2.3025851 * jax.random.uniform(seeds[3], (COMPONENTS,), jnp.float32) ** level_of(seeds[3], (COMPONENTS,), ((0, 8),), -0.2, 0.2)), 0.00234375, 0.0234375),
    }


anneal = 1.0
step_weight = 0.5
ridge_term = 0.01
normal_offset = 0.9189385332046727
exact_mode = lax.Precision.HIGHEST

def reference(vectors, centers, factors, mixing):
    vector_total, features = vectors.shape
    wide_vectors = vectors.astype(jnp.float32)
    identity = jnp.eye(features, dtype=jnp.float32)

    def density(component):
        factor, center = component
        factor_wide = factor.astype(jnp.float32)
        whitened = jnp.dot(vectors.astype(jnp.float32), factor.T.astype(jnp.float32), preferred_element_type=jnp.float32) - jnp.dot(factor_wide, center, precision=exact_mode)[None, :]
        return jnp.sum(jnp.log(jnp.diagonal(factor_wide))) - 0.5 * jnp.sum(whitened * whitened, axis=1)
    log_density = lax.map(density, (factors, centers))
    scores = anneal * (log_density + jnp.log(mixing)[:, None] - features * normal_offset)
    row_max = jnp.max(scores, axis=0)
    exponent = jnp.exp(scores - row_max[None, :])
    col_total = jnp.sum(exponent, axis=0)
    shares = exponent / col_total[None, :]
    evidence = (row_max + jnp.log(col_total)) / anneal

    def update(component):
        factor, center, prior_weight, share_row = component
        counts = jnp.sum(share_row)
        first_moment = jnp.dot(share_row, wide_vectors, precision=exact_mode)
        weighted = share_row[:, None] * wide_vectors
        gram_matrix = jnp.dot(weighted.T, wide_vectors, precision=exact_mode)
        kept_share = (1.0 - step_weight) * prior_weight
        weight = kept_share + step_weight * counts / vector_total
        mean_vector = (kept_share * center + step_weight * first_moment / vector_total) / weight
        moment_part = (kept_share * jnp.outer(center, center) + step_weight * gram_matrix / vector_total) / weight - jnp.outer(mean_vector, mean_vector)
        inverse = lax.linalg.triangular_solve(factor.astype(jnp.float32), identity, left_side=True, lower=True)
        covariance = kept_share / weight * jnp.dot(inverse, inverse.T, precision=exact_mode) + moment_part + ridge_term * identity
        cholesky_factor = jnp.linalg.cholesky(covariance)
        refreshed = lax.linalg.triangular_solve(cholesky_factor, identity, left_side=True, lower=True)
        return (refreshed, mean_vector, weight)
    new_factors, new_means, new_weights = lax.map(update, (factors, centers, mixing, shares))
    return (new_factors, new_means, new_weights, evidence)
```

```python
import functools

import jax
import jax.numpy as jnp
from jax import lax
from jax.experimental import pallas as pl
from jax.experimental.pallas import tpu as pltpu
from jax.sharding import PartitionSpec as P

step_weight = 0.5
ridge_term = 0.01
normal_offset = 0.9189385332046727
panel_rows = 32
lanes = 128
sub = 8
f32 = jnp.float32
bf16 = jnp.bfloat16
both_inner = (((1,), (1,)), ((), ()))
both_outer = (((0,), (0,)), ((), ()))


def split3(value):
    high = value.astype(bf16)
    rest = value - high.astype(f32)
    middle = rest.astype(bf16)
    low = (rest - middle.astype(f32)).astype(bf16)
    return high, middle, low


def product3(left, right, dims, axis):
    lh, lm, ll = left
    rh, rm, rl = right
    return lax.dot_general(
        jnp.concatenate([lh, lh, lh, lm, lm, ll], axis=axis),
        jnp.concatenate([rh, rm, rl, rh, rm, rh], axis=axis),
        dims,
        preferred_element_type=f32,
    )


def diagonal_mask(size):
    return lax.broadcasted_iota(jnp.int32, (size, size), 0) == lax.broadcasted_iota(
        jnp.int32, (size, size), 1
    )


def whiten(factor, everyone, center):
    raw = lax.dot_general(factor, everyone, both_inner, preferred_element_type=f32)
    return raw - jnp.sum(factor.astype(f32) * center, axis=1, keepdims=True)


def score_row(factor, whitened, mix):
    size = factor.shape[0]
    diagonal = jnp.sum(jnp.where(diagonal_mask(size), factor.astype(f32), 0.0), axis=0, keepdims=True)
    log_det = jnp.sum(jnp.log(diagonal), axis=1, keepdims=True)
    density = log_det - 0.5 * jnp.sum(whitened * whitened, axis=0, keepdims=True)
    return density + jnp.log(mix) - size * normal_offset


def middle_matrix(factor, whitened, share, coef, retained):
    size = factor.shape[0]
    q = coef * jnp.sum(whitened * share, axis=1, keepdims=True)
    q_row = jnp.transpose(jnp.broadcast_to(q, (size, lanes)))[0:1, :]
    parts = split3(whitened * jnp.sqrt(coef * share))
    gram = product3(parts, parts, both_inner, 1)
    ridge = ridge_term * lax.dot_general(factor, factor, both_inner, preferred_element_type=f32)
    return jnp.where(diagonal_mask(size), retained, 0.0) + ridge + (gram - q * q_row)


def eliminate(tiles, offset):
    tiles = [list(row) for row in tiles]
    count = len(tiles)
    row_id = lax.broadcasted_iota(jnp.int32, (sub, lanes), 0)
    scales = []
    for chunk in range(count):
        columns = [
            [
                jnp.broadcast_to(
                    tiles[r][0][:, offset + chunk * sub + k : offset + chunk * sub + k + 1], (sub, lanes)
                )
                for r in range(chunk, count)
            ]
            for k in range(sub)
        ]
        scale = jnp.zeros((sub, lanes), f32)
        for k in range(sub):
            pivot = columns[k][0][k : k + 1, :]
            inverse = 1.0 / pivot
            scale = jnp.where(row_id == k, lax.rsqrt(pivot), scale)
            mult = [column * inverse for column in columns[k]]
            mult[0] = jnp.where(row_id > k, mult[0], 0.0)
            for later in range(k + 1, sub):
                row = columns[later][0][k : k + 1, :]
                columns[later] = [c - m * row for c, m in zip(columns[later], mult)]
            for t in range(len(tiles[chunk])):
                row = tiles[chunk][t][k : k + 1, :]
                for r in range(chunk, count):
                    tiles[r][t] = tiles[r][t] - mult[r - chunk] * row
        scales.append(scale)
    return [[tile * scale for tile in row] for row, scale in zip(tiles, scales)]


def factor_panel(panel, size, group, left_ref, right_ref):
    first = panel * panel_rows
    half = first // lanes
    width = size // lanes
    lead = (width - half) * lanes
    finished = []
    for g in range(group):
        tiles = [
            [
                left_ref[g, first + r * sub : first + (r + 1) * sub, t * lanes : (t + 1) * lanes]
                for t in range(half, width)
            ]
            + [
                right_ref[g, first + r * sub : first + (r + 1) * sub, t * lanes : (t + 1) * lanes]
                for t in range(half + 1)
            ]
            for r in range(panel_rows // sub)
        ]
        finished.append(tiles)
    finished = [eliminate(tiles, first - half * lanes) for tiles in finished]
    rows = [jnp.concatenate([jnp.concatenate(row, axis=1) for row in tiles], axis=0) for tiles in finished]
    after = first + panel_rows
    if after < size:
        for g in range(group):
            parts = split3(rows[g])
            update = product3([part[:, :lead] for part in parts], parts, both_outer, 0)
            update = update[after - half * lanes :, :]
            left_ref[g, after:, half * lanes :] -= update[:, :lead]
            right_ref[g, after:, : (half + 1) * lanes] -= update[:, lead:]
    return [row[:, lead:] for row in rows]


def score_kernel(factor_ref, everyone_ref, center_ref, mix_ref, score_ref, stat_ref):
    group = factor_ref.shape[0]
    everyone = everyone_ref[...]
    for g in range(group):
        factor = factor_ref[g]
        whitened = whiten(factor, everyone, center_ref[g : g + 1, :])
        score_ref[g : g + 1, :] = score_row(factor, whitened, mix_ref[g : g + 1, :])
    scores = score_ref[...]
    top = jnp.max(scores, axis=0, keepdims=True)
    stat_ref[0:1, :] = top
    stat_ref[1:2, :] = jnp.sum(jnp.exp(scores - top), axis=0, keepdims=True)


def update_kernel(
    factor_ref, everyone_ref, center_ref, mix_ref, score_ref, tops_ref, totals_ref,
    fresh_ref, mean_ref, weight_ref, evidence_ref, left_ref, right_ref,
):
    group, size, unused = factor_ref.shape
    everyone = everyone_ref[...]
    total_vectors = everyone.shape[0]
    tops = tops_ref[...]
    top = jnp.max(tops, axis=0, keepdims=True)
    total = jnp.sum(totals_ref[...] * jnp.exp(tops - top), axis=0, keepdims=True)
    evidence_ref[...] = top + jnp.log(total)
    shares = jnp.exp(score_ref[...] - top) / total
    counts = jnp.sum(shares, axis=1, keepdims=True)
    first_moment = sum(
        jnp.dot(part, everyone, preferred_element_type=f32) for part in split3(shares)
    )
    kept = (1.0 - step_weight) * mix_ref[...]
    weights = kept + step_weight * counts / total_vectors
    weight_ref[...] = weights
    mean_ref[...] = (kept * center_ref[...] + step_weight * first_moment / total_vectors) / weights
    retained = kept / weights
    coef = step_weight / (total_vectors * weights)
    for g in range(group):
        factor = factor_ref[g]
        whitened = whiten(factor, everyone, center_ref[g : g + 1, :])
        left_ref[g] = middle_matrix(
            factor, whitened, shares[g : g + 1, :], coef[g : g + 1, :], retained[g : g + 1, :]
        )
        right_ref[g] = factor.astype(f32)
    for panel in range(size // panel_rows):
        rows = factor_panel(panel, size, group, left_ref, right_ref)
        first = panel * panel_rows
        for g in range(group):
            filled = rows[g].shape[1]
            fresh_ref[g, first : first + panel_rows, :filled] = rows[g]
            if filled < size:
                fresh_ref[g, first : first + panel_rows, filled:] = jnp.zeros(
                    (panel_rows, size - filled), f32
                )


def local(vectors, centers, factors, mixing):
    comp_count, row_count, features = factors.shape
    groups = lax.axis_size("dp")
    owned = comp_count // groups
    position = lax.axis_index("dp")
    row_start = position * owned
    everyone = lax.all_gather(vectors, "dp", axis=0, tiled=True)
    total_vectors = everyone.shape[0]
    whole = lax.all_to_all(
        factors.reshape(groups, owned, row_count, features), "dp", split_axis=0, concat_axis=2, tiled=True
    ).reshape(owned, features, features)
    own_centers = lax.dynamic_slice_in_dim(centers, row_start, owned, 0)
    own_mixing = lax.dynamic_slice_in_dim(mixing, row_start, owned, 0)[:, None]
    params = pltpu.CompilerParams(vmem_limit_bytes=48 * 1024 * 1024)
    scores, stats = pl.pallas_call(
        score_kernel,
        out_shape=(
            jax.ShapeDtypeStruct((owned, total_vectors), f32),
            jax.ShapeDtypeStruct((2, total_vectors), f32),
        ),
        compiler_params=params,
    )(whole, everyone, own_centers, own_mixing)
    gathered = lax.all_gather(stats, ("dp", "comp"), axis=1)
    fresh, means, weights, evidence = pl.pallas_call(
        update_kernel,
        out_shape=(
            jax.ShapeDtypeStruct((owned, features, features), f32),
            jax.ShapeDtypeStruct((owned, features), f32),
            jax.ShapeDtypeStruct((owned, 1), f32),
            jax.ShapeDtypeStruct((1, total_vectors), f32),
        ),
        scratch_shapes=[pltpu.VMEM((owned, features, features), f32)] * 2,
        compiler_params=params,
    )(whole, everyone, own_centers, own_mixing, scores, gathered[0], gathered[1])
    new_factors = lax.all_to_all(
        fresh[None], "dp", split_axis=2, concat_axis=0, tiled=True
    ).reshape(comp_count, row_count, features)
    packed = jnp.concatenate([means, jnp.broadcast_to(weights, (owned, lanes))], axis=1)
    packed = lax.all_gather(packed, "dp", axis=0, tiled=True)
    count = vectors.shape[0]
    own_evidence = lax.dynamic_slice_in_dim(evidence[0], position * count, count, 0)
    return new_factors, packed[:, :features], packed[:, features], own_evidence


def solution(mesh):
    return jax.shard_map(
        local,
        mesh=mesh,
        in_specs=(P("dp", None), P("comp", None), P("comp", "dp", None), P("comp")),
        out_specs=(P("comp", "dp", None), P("comp", None), P("comp"), P("dp")),
        check_vma=False,
    )
```

```python
import functools

import jax
import jax.numpy as jnp
from jax import lax
from jax.experimental import pallas as pl
from jax.experimental.pallas import tpu as pltpu
from jax.sharding import PartitionSpec as P

step_weight = 0.5
ridge_term = 0.01
normal_offset = 0.9189385332046727
panel_rows = 32
lanes = 128
sub = 8
f32 = jnp.float32
bf16 = jnp.bfloat16
both_inner = (((1,), (1,)), ((), ()))
both_outer = (((0,), (0,)), ((), ()))


def split3(value):
    high = value.astype(bf16)
    rest = value - high.astype(f32)
    middle = rest.astype(bf16)
    low = (rest - middle.astype(f32)).astype(bf16)
    return high, middle, low


def product3(left, right, dims, axis):
    lh, lm, ll = left
    rh, rm, rl = right
    return lax.dot_general(
        jnp.concatenate([lh, lh, lh, lm, lm, ll], axis=axis),
        jnp.concatenate([rh, rm, rl, rh, rm, rh], axis=axis),
        dims,
        preferred_element_type=f32,
    )


def diagonal_mask(size):
    return lax.broadcasted_iota(jnp.int32, (size, size), 0) == lax.broadcasted_iota(
        jnp.int32, (size, size), 1
    )


def whiten(factor, everyone, center):
    raw = lax.dot_general(factor, everyone, both_inner, preferred_element_type=f32)
    return raw - jnp.sum(factor.astype(f32) * center, axis=1, keepdims=True)


def score_row(factor, whitened, mix):
    size = factor.shape[0]
    diagonal = jnp.sum(jnp.where(diagonal_mask(size), factor.astype(f32), 0.0), axis=0, keepdims=True)
    log_det = jnp.sum(jnp.log(diagonal), axis=1, keepdims=True)
    density = log_det - 0.5 * jnp.sum(whitened * whitened, axis=0, keepdims=True)
    return density + jnp.log(mix) - size * normal_offset


def add_moment(left, whitened, share, coef, retained):
    size = left.shape[0]
    q = coef * jnp.sum(whitened * share, axis=1, keepdims=True)
    q_row = jnp.transpose(jnp.broadcast_to(q, (size, lanes)))[0:1, :]
    parts = split3(whitened * jnp.sqrt(coef * share))
    gram = product3(parts, parts, both_inner, 1)
    return jnp.where(diagonal_mask(size), retained, 0.0) + left + (gram - q * q_row)


def eliminate(tiles, offset):
    tiles = [list(row) for row in tiles]
    count = len(tiles)
    row_id = lax.broadcasted_iota(jnp.int32, (sub, lanes), 0)
    scales = []
    for chunk in range(count):
        columns = [
            [
                jnp.broadcast_to(
                    tiles[r][0][:, offset + chunk * sub + k : offset + chunk * sub + k + 1], (sub, lanes)
                )
                for r in range(chunk, count)
            ]
            for k in range(sub)
        ]
        scale = jnp.zeros((sub, lanes), f32)
        for k in range(sub):
            pivot = columns[k][0][k : k + 1, :]
            inverse = 1.0 / pivot
            scale = jnp.where(row_id == k, lax.rsqrt(pivot), scale)
            mult = [column * inverse for column in columns[k]]
            mult[0] = jnp.where(row_id > k, mult[0], 0.0)
            for later in range(k + 1, sub):
                row = columns[later][0][k : k + 1, :]
                columns[later] = [c - m * row for c, m in zip(columns[later], mult)]
            for t in range(len(tiles[chunk])):
                row = tiles[chunk][t][k : k + 1, :]
                for r in range(chunk, count):
                    tiles[r][t] = tiles[r][t] - mult[r - chunk] * row
        scales.append(scale)
    return [[tile * scale for tile in row] for row, scale in zip(tiles, scales)]


def factor_panel(panel, size, group, left_ref, right_ref):
    first = panel * panel_rows
    half = first // lanes
    width = size // lanes
    lead = (width - half) * lanes
    finished = []
    for g in range(group):
        tiles = [
            [
                left_ref[g, first + r * sub : first + (r + 1) * sub, t * lanes : (t + 1) * lanes]
                for t in range(half, width)
            ]
            + [
                right_ref[g, first + r * sub : first + (r + 1) * sub, t * lanes : (t + 1) * lanes]
                for t in range(half + 1)
            ]
            for r in range(panel_rows // sub)
        ]
        finished.append(tiles)
    finished = [eliminate(tiles, first - half * lanes) for tiles in finished]
    rows = [jnp.concatenate([jnp.concatenate(row, axis=1) for row in tiles], axis=0) for tiles in finished]
    after = first + panel_rows
    if after < size:
        for g in range(group):
            parts = split3(rows[g])
            update = product3([part[:, :lead] for part in parts], parts, both_outer, 0)
            update = update[after - half * lanes :, :]
            left_ref[g, after:, half * lanes :] -= update[:, :lead]
            right_ref[g, after:, : (half + 1) * lanes] -= update[:, lead:]
    return [row[:, lead:] for row in rows]


def merge(slots_ref):
    count = slots_ref.shape[0]
    tops = [slots_ref[i, 0:1, :] for i in range(count)]
    top = functools.reduce(jnp.maximum, tops)
    return top, sum(slots_ref[i, 1:2, :] * jnp.exp(tops[i] - top) for i in range(count))


def remote(source, target, send_sem, recv_sem, axis, peer):
    return pltpu.make_async_remote_copy(
        src_ref=source,
        dst_ref=target,
        send_sem=send_sem,
        recv_sem=recv_sem,
        device_id={axis: peer},
        device_id_type=pl.DeviceIdType.MESH,
    )


def spread(groups, position, axis, kind, sends, receives, source_of, target):
    copies = []
    for step in range(1, groups):
        peer = lax.rem(position + step, groups)
        copy = remote(
            source_of(peer), target, sends.at[kind, step], receives.at[kind, step], axis, peer
        )
        copy.start()
        copies.append(copy)
    return copies


def finish(copies):
    for copy in copies:
        copy.wait()


def step_kernel(
    groups, comps,
    vectors_ref, factors_ref, center_ref, mix_ref,
    out_ref, packed_ref, evidence_ref,
    everyone_ref, whole_ref, score_ref, white_ref, left_ref, right_ref, fresh_ref,
    comp_slots, dp_slots, sends, receives, comp_sends, comp_receives, out_sends, out_receives,
):
    position = lax.axis_index("dp")
    column = lax.axis_index("comp")
    unused, group, rows, size = factors_ref.shape
    local_vectors = vectors_ref.shape[0]
    total_vectors = groups * local_vectors

    barrier = pltpu.get_barrier_semaphore()
    for axis, place, count in (("dp", position, groups), ("comp", column, comps)):
        for step in range(1, count):
            pl.semaphore_signal(
                barrier, inc=1, device_id={axis: lax.rem(place + step, count)},
                device_id_type=pl.DeviceIdType.MESH,
            )
    pl.semaphore_wait(barrier, groups + comps - 2)

    vector_copies = spread(
        groups, position, "dp", 0, sends, receives, lambda peer: vectors_ref, everyone_ref.at[position]
    )
    factor_copies = spread(
        groups, position, "dp", 1, sends, receives,
        lambda peer: factors_ref.at[peer], whole_ref.at[:, position],
    )
    everyone_ref[position] = vectors_ref[...]
    for g in range(group):
        whole_ref[g, position] = factors_ref[position, g]
    for tile in range(1, size // lanes):
        @pl.when((position + 1) * rows <= tile * lanes)
        def clear():
            out_ref[:, :, :, tile * lanes : (tile + 1) * lanes] = jnp.zeros(
                (groups, group, rows, lanes), f32
            )
    finish(vector_copies)
    finish(factor_copies)

    everyone = everyone_ref[...].reshape(total_vectors, size)
    for g in range(group):
        factor = whole_ref[g].reshape(size, size)
        whitened = whiten(factor, everyone, center_ref[g : g + 1, :])
        white_ref[g] = whitened
        score_ref[g : g + 1, :] = score_row(factor, whitened, mix_ref[g : g + 1, :])
    scores = score_ref[...]
    top = jnp.max(scores, axis=0, keepdims=True)
    comp_slots[column, 0:1, :] = top
    comp_slots[column, 1:2, :] = jnp.sum(jnp.exp(scores - top), axis=0, keepdims=True)
    copies = spread(
        comps, column, "comp", 0, comp_sends, comp_receives,
        lambda peer: comp_slots.at[column], comp_slots.at[column],
    )
    for g in range(group):
        factor = whole_ref[g].reshape(size, size)
        left_ref[g] = ridge_term * lax.dot_general(
            factor, factor, both_inner, preferred_element_type=f32
        )
        right_ref[g] = factor.astype(f32)
    finish(copies)
    top, total = merge(comp_slots)
    dp_slots[position, 0:1, :] = top
    dp_slots[position, 1:2, :] = total
    finish(spread(
        groups, position, "dp", 2, sends, receives,
        lambda peer: dp_slots.at[position], dp_slots.at[position],
    ))
    top, total = merge(dp_slots)
    evidence_ref[...] = top + jnp.log(total)

    shares = jnp.exp(score_ref[...] - top) / total
    counts = jnp.sum(shares, axis=1, keepdims=True)
    first_moment = sum(
        jnp.dot(part, everyone, preferred_element_type=f32) for part in split3(shares)
    )
    kept = (1.0 - step_weight) * mix_ref[...]
    weights = kept + step_weight * counts / total_vectors
    means = (kept * center_ref[...] + step_weight * first_moment / total_vectors) / weights
    packed_ref[position] = jnp.concatenate([means, jnp.broadcast_to(weights, (group, lanes))], axis=1)
    mean_copies = spread(
        groups, position, "dp", 3, sends, receives,
        lambda peer: packed_ref.at[position], packed_ref.at[position],
    )
    retained = kept / weights
    coef = step_weight / (total_vectors * weights)
    for g in range(group):
        left_ref[g] = add_moment(
            left_ref[g], white_ref[g], shares[g : g + 1, :], coef[g : g + 1, :], retained[g : g + 1, :]
        )

    def width(target):
        return -(-(target + 1) * rows // lanes) * lanes

    def result_copy(source, target):
        return remote(
            fresh_ref.at[:, target * rows : (target + 1) * rows, : width(target)],
            out_ref.at[source, :, :, : width(target)],
            out_sends.at[target], out_receives.at[source], "dp", target,
        )

    sent = 0
    for panel in range(size // panel_rows):
        done = factor_panel(panel, size, group, left_ref, right_ref)
        first = panel * panel_rows
        for g in range(group):
            fresh_ref[g, first : first + panel_rows, : done[g].shape[1]] = done[g]
        while (sent + 1) * rows <= first + panel_rows:
            target = sent

            @pl.when(position != target)
            def send():
                result_copy(position, target).start()

            @pl.when(position == target)
            def keep():
                for g in range(group):
                    out_ref[target, g, :, : width(target)] = fresh_ref[
                        g, target * rows : (target + 1) * rows, : width(target)
                    ]

            sent += 1
    for target in range(groups):
        @pl.when(position != target)
        def drain():
            result_copy(position, target).wait_send()

        @pl.when(position == target)
        def collect():
            for source in range(groups):
                if source != target:
                    result_copy(source, target).wait_recv()

    finish(mean_copies)


def local(vectors, centers, factors, mixing):
    comp_count, row_count, features = factors.shape
    groups, comps = lax.axis_size("dp"), lax.axis_size("comp")
    owned = comp_count // groups
    position = lax.axis_index("dp")
    local_vectors = vectors.shape[0]
    total_vectors = local_vectors * groups
    own_centers = lax.dynamic_slice_in_dim(centers, position * owned, owned, 0)
    own_mixing = lax.dynamic_slice_in_dim(mixing, position * owned, owned, 0)[:, None]
    dma = pltpu.SemaphoreType.DMA
    in_vmem = pl.BlockSpec(memory_space=pltpu.VMEM)
    fresh, packed, evidence = pl.pallas_call(
        functools.partial(step_kernel, groups, comps),
        out_shape=(
            jax.ShapeDtypeStruct((groups, owned, row_count, features), f32),
            jax.ShapeDtypeStruct((groups, owned, features + lanes), f32),
            jax.ShapeDtypeStruct((1, total_vectors), f32),
        ),
        in_specs=[in_vmem] * 4,
        out_specs=(in_vmem,) * 3,
        scratch_shapes=[
            pltpu.VMEM((groups, local_vectors, features), bf16),
            pltpu.VMEM((owned, groups, row_count, features), bf16),
            pltpu.VMEM((owned, total_vectors), f32),
            pltpu.VMEM((owned, features, total_vectors), f32),
            pltpu.VMEM((owned, features, features), f32),
            pltpu.VMEM((owned, features, features), f32),
            pltpu.VMEM((owned, features, features), f32),
            pltpu.VMEM((comps, 2, total_vectors), f32),
            pltpu.VMEM((groups, 2, total_vectors), f32),
            dma((4, groups)), dma((4, groups)),
            dma((1, comps)), dma((1, comps)),
            dma((groups,)), dma((groups,)),
        ],
        compiler_params=pltpu.CompilerParams(
            collective_id=0, has_side_effects=True, vmem_limit_bytes=48 * 1024 * 1024
        ),
    )(vectors, factors.reshape(groups, owned, row_count, features), own_centers, own_mixing)
    packed = packed.reshape(comp_count, features + lanes)
    own_evidence = lax.dynamic_slice_in_dim(evidence[0], position * local_vectors, local_vectors, 0)
    return (
        fresh.reshape(comp_count, row_count, features),
        packed[:, :features], packed[:, features], own_evidence,
    )


def solution(mesh):
    return jax.shard_map(
        local,
        mesh=mesh,
        in_specs=(P("dp", None), P("comp", None), P("comp", "dp", None), P("comp")),
        out_specs=(P("comp", "dp", None), P("comp", None), P("comp"), P("dp")),
        check_vma=False,
    )
```

```python
import functools

import jax
import jax.numpy as jnp
from jax import lax
from jax.experimental import pallas as pl
from jax.experimental.pallas import tpu as pltpu
from jax.sharding import PartitionSpec as P

step_weight = 0.5
ridge_term = 0.01
normal_offset = 0.9189385332046727
panel_rows = 32
lanes = 128
sub = 8
f32 = jnp.float32
bf16 = jnp.bfloat16
both_inner = (((1,), (1,)), ((), ()))
both_outer = (((0,), (0,)), ((), ()))


def split3(value):
    high = value.astype(bf16)
    rest = value - high.astype(f32)
    middle = rest.astype(bf16)
    low = (rest - middle.astype(f32)).astype(bf16)
    return high, middle, low


def product3(left, right, dims, axis):
    lh, lm, ll = left
    rh, rm, rl = right
    return lax.dot_general(
        jnp.concatenate([lh, lh, lh, lm, lm, ll], axis=axis),
        jnp.concatenate([rh, rm, rl, rh, rm, rh], axis=axis),
        dims,
        preferred_element_type=f32,
    )


def diagonal_mask(size):
    return lax.broadcasted_iota(jnp.int32, (size, size), 0) == lax.broadcasted_iota(
        jnp.int32, (size, size), 1
    )


def whiten(factor, everyone, center):
    raw = lax.dot_general(factor, everyone, both_inner, preferred_element_type=f32)
    return raw - jnp.sum(factor.astype(f32) * center, axis=1, keepdims=True)


def score_row(factor, whitened, mix):
    size = factor.shape[0]
    diagonal = jnp.sum(jnp.where(diagonal_mask(size), factor.astype(f32), 0.0), axis=0, keepdims=True)
    log_det = jnp.sum(jnp.log(diagonal), axis=1, keepdims=True)
    density = log_det - 0.5 * jnp.sum(whitened * whitened, axis=0, keepdims=True)
    return density + jnp.log(mix) - size * normal_offset


def add_moment(left, whitened, share, coef, retained):
    size = left.shape[0]
    q = coef * jnp.sum(whitened * share, axis=1, keepdims=True)
    q_row = jnp.transpose(jnp.broadcast_to(q, (size, lanes)))[0:1, :]
    parts = split3(whitened * jnp.sqrt(coef * share))
    gram = product3(parts, parts, both_inner, 1)
    return jnp.where(diagonal_mask(size), retained, 0.0) + left + (gram - q * q_row)


def eliminate(tiles, offset):
    tiles = [list(row) for row in tiles]
    count = len(tiles)
    row_id = lax.broadcasted_iota(jnp.int32, (sub, lanes), 0)
    scales = []
    for chunk in range(count):
        columns = [
            [
                jnp.broadcast_to(
                    tiles[r][0][:, offset + chunk * sub + k : offset + chunk * sub + k + 1], (sub, lanes)
                )
                for r in range(chunk, count)
            ]
            for k in range(sub)
        ]
        scale = jnp.zeros((sub, lanes), f32)
        for k in range(sub):
            pivot = columns[k][0][k : k + 1, :]
            inverse = 1.0 / pivot
            scale = jnp.where(row_id == k, lax.rsqrt(pivot), scale)
            mult = [column * inverse for column in columns[k]]
            mult[0] = jnp.where(row_id > k, mult[0], 0.0)
            for later in range(k + 1, sub):
                row = columns[later][0][k : k + 1, :]
                columns[later] = [c - m * row for c, m in zip(columns[later], mult)]
            for t in range(len(tiles[chunk])):
                row = tiles[chunk][t][k : k + 1, :]
                for r in range(chunk, count):
                    tiles[r][t] = tiles[r][t] - mult[r - chunk] * row
        scales.append(scale)
    return [[tile * scale for tile in row] for row, scale in zip(tiles, scales)]


def factor_panel(panel, size, group, left_ref, right_ref):
    first = panel * panel_rows
    half = first // lanes
    width = size // lanes
    lead = (width - half) * lanes
    finished = []
    for g in range(group):
        tiles = [
            [
                left_ref[g, first + r * sub : first + (r + 1) * sub, t * lanes : (t + 1) * lanes]
                for t in range(half, width)
            ]
            + [
                right_ref[g, first + r * sub : first + (r + 1) * sub, t * lanes : (t + 1) * lanes]
                for t in range(half + 1)
            ]
            for r in range(panel_rows // sub)
        ]
        finished.append(tiles)
    finished = [eliminate(tiles, first - half * lanes) for tiles in finished]
    rows = [jnp.concatenate([jnp.concatenate(row, axis=1) for row in tiles], axis=0) for tiles in finished]
    after = first + panel_rows
    if after < size:
        for g in range(group):
            parts = split3(rows[g])
            update = product3([part[:, :lead] for part in parts], parts, both_outer, 0)
            update = update[after - half * lanes :, :]
            left_ref[g, after:, half * lanes :] -= update[:, :lead]
            right_ref[g, after:, : (half + 1) * lanes] -= update[:, lead:]
    return [row[:, lead:] for row in rows]


def merge(slots_ref):
    count = slots_ref.shape[0]
    tops = [slots_ref[i, 0:1, :] for i in range(count)]
    top = functools.reduce(jnp.maximum, tops)
    return top, sum(slots_ref[i, 1:2, :] * jnp.exp(tops[i] - top) for i in range(count))


def remote(source, target, send_sem, recv_sem, axis, peer):
    return pltpu.make_async_remote_copy(
        src_ref=source,
        dst_ref=target,
        send_sem=send_sem,
        recv_sem=recv_sem,
        device_id={axis: peer},
        device_id_type=pl.DeviceIdType.MESH,
    )


def spread(groups, position, axis, kind, sends, receives, source_of, target):
    copies = []
    for step in range(1, groups):
        peer = lax.rem(position + step, groups)
        copy = remote(
            source_of(peer), target, sends.at[kind, step], receives.at[kind, step], axis, peer
        )
        copy.start()
        copies.append(copy)
    return copies


def finish(copies):
    for copy in copies:
        copy.wait()


def step_kernel(
    groups, comps,
    vectors_ref, factors_ref, center_ref, mix_ref,
    out_ref, packed_ref, evidence_ref,
    everyone_ref, whole_ref, score_ref, white_ref, left_ref, right_ref, fresh_ref,
    comp_slots, dp_slots, sends, receives, comp_sends, comp_receives, out_sends, out_receives,
):
    position = lax.axis_index("dp")
    column = lax.axis_index("comp")
    unused, group, rows, size = factors_ref.shape
    local_vectors = vectors_ref.shape[0]
    total_vectors = groups * local_vectors

    barrier = pltpu.get_barrier_semaphore()
    for axis, place, count in (("dp", position, groups), ("comp", column, comps)):
        for step in range(1, count):
            pl.semaphore_signal(
                barrier, inc=1, device_id={axis: lax.rem(place + step, count)},
                device_id_type=pl.DeviceIdType.MESH,
            )
    pl.semaphore_wait(barrier, groups + comps - 2)

    vector_copies = spread(
        groups, position, "dp", 0, sends, receives, lambda peer: vectors_ref, everyone_ref.at[position]
    )
    factor_copies = spread(
        groups, position, "dp", 1, sends, receives,
        lambda peer: factors_ref.at[peer], whole_ref.at[:, position],
    )
    everyone_ref[position] = vectors_ref[...]
    for g in range(group):
        whole_ref[g, position] = factors_ref[position, g]
    for tile in range(1, size // lanes):
        @pl.when((position + 1) * rows <= tile * lanes)
        def clear():
            out_ref[:, :, :, tile * lanes : (tile + 1) * lanes] = jnp.zeros(
                (groups, group, rows, lanes), f32
            )
    finish(vector_copies)
    finish(factor_copies)

    everyone = everyone_ref[...].reshape(total_vectors, size)
    for g in range(group):
        factor = whole_ref[g].reshape(size, size)
        whitened = whiten(factor, everyone, center_ref[g : g + 1, :])
        white_ref[g] = whitened
        score_ref[g : g + 1, :] = score_row(factor, whitened, mix_ref[g : g + 1, :])
    scores = score_ref[...]
    top = jnp.max(scores, axis=0, keepdims=True)
    comp_slots[column, 0:1, :] = top
    comp_slots[column, 1:2, :] = jnp.sum(jnp.exp(scores - top), axis=0, keepdims=True)
    copies = spread(
        comps, column, "comp", 0, comp_sends, comp_receives,
        lambda peer: comp_slots.at[column], comp_slots.at[column],
    )
    for g in range(group):
        factor = whole_ref[g].reshape(size, size)
        left_ref[g] = ridge_term * lax.dot_general(
            factor, factor, both_inner, preferred_element_type=f32
        )
        right_ref[g] = factor.astype(f32)
    finish(copies)
    top, total = merge(comp_slots)
    dp_slots[position, 0:1, :] = top
    dp_slots[position, 1:2, :] = total
    finish(spread(
        groups, position, "dp", 2, sends, receives,
        lambda peer: dp_slots.at[position], dp_slots.at[position],
    ))
    top, total = merge(dp_slots)
    evidence_ref[...] = top + jnp.log(total)

    shares = jnp.exp(score_ref[...] - top) / total
    counts = jnp.sum(shares, axis=1, keepdims=True)
    first_moment = sum(
        jnp.dot(part, everyone, preferred_element_type=f32) for part in split3(shares)
    )
    kept = (1.0 - step_weight) * mix_ref[...]
    weights = kept + step_weight * counts / total_vectors
    means = (kept * center_ref[...] + step_weight * first_moment / total_vectors) / weights
    packed_ref[position] = jnp.concatenate([means, jnp.broadcast_to(weights, (group, lanes))], axis=1)
    mean_copies = spread(
        groups, position, "dp", 3, sends, receives,
        lambda peer: packed_ref.at[position], packed_ref.at[position],
    )
    retained = kept / weights
    coef = step_weight / (total_vectors * weights)
    for g in range(group):
        left_ref[g] = add_moment(
            left_ref[g], white_ref[g], shares[g : g + 1, :], coef[g : g + 1, :], retained[g : g + 1, :]
        )

    def width(target):
        return -(-(target + 1) * rows // lanes) * lanes

    unit = min(panel_rows, rows)
    pieces = rows // unit

    def result_copy(source, target, piece):
        start = target * rows + piece * unit
        return remote(
            fresh_ref.at[:, start : start + unit, : width(target)],
            out_ref.at[source, :, piece * unit : (piece + 1) * unit, : width(target)],
            out_sends.at[target, piece], out_receives.at[source, piece], "dp", target,
        )

    sent = 0
    for panel in range(size // panel_rows):
        done = factor_panel(panel, size, group, left_ref, right_ref)
        first = panel * panel_rows
        for g in range(group):
            fresh_ref[g, first : first + panel_rows, : done[g].shape[1]] = done[g]
        while (sent + 1) * unit <= first + panel_rows:
            target, piece = divmod(sent, pieces)
            start = sent * unit

            @pl.when(position != target)
            def send():
                result_copy(position, target, piece).start()

            @pl.when(position == target)
            def keep():
                for g in range(group):
                    out_ref[target, g, piece * unit : (piece + 1) * unit, : width(target)] = fresh_ref[
                        g, start : start + unit, : width(target)
                    ]

            sent += 1
    for target in range(groups):
        @pl.when(position != target)
        def drain():
            for piece in range(pieces):
                result_copy(position, target, piece).wait_send()

        @pl.when(position == target)
        def collect():
            for source in range(groups):
                if source != target:
                    for piece in range(pieces):
                        result_copy(source, target, piece).wait_recv()

    finish(mean_copies)


def local(vectors, centers, factors, mixing):
    comp_count, row_count, features = factors.shape
    groups, comps = lax.axis_size("dp"), lax.axis_size("comp")
    owned = comp_count // groups
    position = lax.axis_index("dp")
    local_vectors = vectors.shape[0]
    total_vectors = local_vectors * groups
    own_centers = lax.dynamic_slice_in_dim(centers, position * owned, owned, 0)
    own_mixing = lax.dynamic_slice_in_dim(mixing, position * owned, owned, 0)[:, None]
    dma = pltpu.SemaphoreType.DMA
    in_vmem = pl.BlockSpec(memory_space=pltpu.VMEM)
    fresh, packed, evidence = pl.pallas_call(
        functools.partial(step_kernel, groups, comps),
        out_shape=(
            jax.ShapeDtypeStruct((groups, owned, row_count, features), f32),
            jax.ShapeDtypeStruct((groups, owned, features + lanes), f32),
            jax.ShapeDtypeStruct((1, total_vectors), f32),
        ),
        in_specs=[in_vmem] * 4,
        out_specs=(in_vmem,) * 3,
        scratch_shapes=[
            pltpu.VMEM((groups, local_vectors, features), bf16),
            pltpu.VMEM((owned, groups, row_count, features), bf16),
            pltpu.VMEM((owned, total_vectors), f32),
            pltpu.VMEM((owned, features, total_vectors), f32),
            pltpu.VMEM((owned, features, features), f32),
            pltpu.VMEM((owned, features, features), f32),
            pltpu.VMEM((owned, features, features), f32),
            pltpu.VMEM((comps, 2, total_vectors), f32),
            pltpu.VMEM((groups, 2, total_vectors), f32),
            dma((4, groups)), dma((4, groups)),
            dma((1, comps)), dma((1, comps)),
            dma((groups, row_count // min(panel_rows, row_count))),
            dma((groups, row_count // min(panel_rows, row_count))),
        ],
        compiler_params=pltpu.CompilerParams(
            collective_id=0, has_side_effects=True, vmem_limit_bytes=48 * 1024 * 1024
        ),
    )(vectors, factors.reshape(groups, owned, row_count, features), own_centers, own_mixing)
    packed = packed.reshape(comp_count, features + lanes)
    own_evidence = lax.dynamic_slice_in_dim(evidence[0], position * local_vectors, local_vectors, 0)
    return (
        fresh.reshape(comp_count, row_count, features),
        packed[:, :features], packed[:, features], own_evidence,
    )


def solution(mesh):
    return jax.shard_map(
        local,
        mesh=mesh,
        in_specs=(P("dp", None), P("comp", None), P("comp", "dp", None), P("comp")),
        out_specs=(P("comp", "dp", None), P("comp", None), P("comp"), P("dp")),
        check_vma=False,
    )
```
